32 devices in a mesh: dp: 4 (over z), owner: 8 (over y, x, core).
Axes of the slice: x: 2, y: 2, z: 4, core: 2. Of those that a mesh axis runs over, the one named last changes fastest.
Arguments:
- tokens: bfloat16 [4096, 8192], P(('dp', 'owner')), may hold values from -6 to 6
- residual: bfloat16 [4096, 8192], P(('dp', 'owner')), may hold values from -6 to 6
- token_adapter_index: int32 [4096, 1], P(('dp', 'owner')), may hold values from 0 to 7; in each aligned block of 128 rows (0 to 127, 128 to 255, ...) at most 24 rows name the same one
- adapter_down_weight: bfloat16 [8, 64, 8192], P('owner', None, 'dp'), may hold values from -0.0625 to 0.0625
- adapter_up_weight: bfloat16 [8, 64, 8192], P('owner', None, 'dp'), may hold values from -0.75 to 0.75
- down_moment_first: bfloat16 [8, 64, 8192], P('owner', None, 'dp'), may hold values from -135 to 135
- down_moment_second: bfloat16 [8, 64, 8192], P('owner', None, 'dp'), may hold values from 204 to 6144
- up_moment_first: bfloat16 [8, 64, 8192], P('owner', None, 'dp'), may hold values from -13.5625 to 13.5625
- up_moment_second: bfloat16 [8, 64, 8192], P('owner', None, 'dp'), may hold values from 1.53125 to 51
Outputs:
- down_update: float32 [8, 64, 8192], P('owner', None, 'dp')
- up_update: float32 [8, 64, 8192], P('owner', None, 'dp')
- token_loss: float32 [4096], P(('dp', 'owner'))
The draws below stay inside these ranges and needn't reach their ends.
Inputs may be any that keep to these rules, and one draw needn't show every extreme that they name: `token_adapter_index`: of the 128 rows of one device, at most 24 name one adapter, and in some devices one adapter is named by exactly 24.
All inputs are finite; a program needn't handle non-finite values.
Results may differ from the reference program's by a relative error of at most 0.0091.
Values may be sent and summed in bfloat16 or wider, within the bound.
A program may use at most 128 MiB of HBM per device.

```python
import math
import jax
import jax.numpy as jnp
import numpy as np
from jax import lax

MODEL_DIM = 8192
ADAPTER_RANK = 64
TOK_DEV = 128
ADAPTER_COUNT = 8
TOKENS = 4096
MOST = 24
TENANT_ROWS = 512
N_DP = 4
N_OWNER = 8


def level_of(rng, extent, split, least, top_value):
    level, own = 1.0, jax.random.fold_in(rng, 6)
    for axis_at, shards_of in split:
        steps = jnp.exp(jax.random.uniform(jax.random.fold_in(own, axis_at), (shards_of,), jnp.float32, least / len(split), top_value / len(split)))
        level = level * jnp.repeat(steps, extent[axis_at] // shards_of).reshape([-1 if axis == axis_at else 1 for axis in range(len(extent))])
    return level


def routed_block(rng, own, number, rows, amount, top, limit, lean):
    order = jax.random.permutation(rng, amount)
    crowded, usual = shares(amount, rows * top, limit, lean, True), shares(amount, rows * top, limit, lean, False)
    places = jnp.arange(amount)

    def named(sizes, turn):
        used = int((sizes > 0).sum())
        fixed = max(1, used // 4)
        shifted = fixed + (places - fixed + turn * (used - fixed)) % max(1, amount - fixed)
        return jnp.zeros((amount,), jnp.int32).at[order[jnp.where(places < fixed, places, shifted)]].set(jnp.asarray(sizes, jnp.int32))

    sizes = jnp.where(number % 4 == 0, named(crowded, number // 4), named(usual, number - number // 4 - 1))
    mixed = jax.random.permutation(jax.random.fold_in(own, 3), amount)
    giver, sink = mixed[0:amount // 2 * 2:2], mixed[1:amount // 2 * 2:2]
    room = jnp.minimum(sizes[giver] - 1, limit - sizes[sink]) // 2
    room = jnp.where((giver == order[0]) | (sink == order[0]) | (sizes[sink] == 0), 0, jnp.maximum(room, 0))
    shifted = jax.random.randint(jax.random.fold_in(own, 4), (amount // 2,), 0, 1 << 20) % (room + 1)
    sizes = sizes.at[giver].add(-shifted).at[sink].add(shifted)
    members = jnp.searchsorted(jnp.cumsum(sizes), jnp.arange(rows * top), side="right").astype(jnp.int32)
    table = members.reshape(top, rows).T
    table = table[jax.random.permutation(jax.random.fold_in(own, 1), rows)]
    turn = jax.random.randint(jax.random.fold_in(own, 2), (rows, 1), 0, top)
    return jnp.take_along_axis(table, (jnp.arange(top)[None, :] + turn) % top, axis=1)


def shares(amount, total, most, skew, full):
    weights = [(1 << 20) // math.isqrt(grade ** skew) + 1 for grade in range(1, amount + 1)]
    largest = most if full else min(most, max(-(-total // amount), total * weights[0] // sum(weights)))
    least = 1 if total - largest >= amount - 1 else 0
    given, spare = [largest] + [least] * (amount - 1), total - largest - least * (amount - 1)
    while spare > 0:
        candidates = [i for i in range(1, amount) if given[i] < largest] or [i for i in range(1, amount) if given[i] < most]
        pool, left = sum([weights[i] for i in candidates]), spare
        for i in candidates:
            extra = min(most - given[i], max(1, left * weights[i] // pool), spare)
            given[i] = given[i] + extra
            spare = spare - extra
    return np.array(given)


def scatter_about(own_key, dims, spread, limit, split=(), held_as=jnp.bfloat16):
    gain = level_of(own_key, dims, split, -0.22, 0.18) if split else 1.0
    result = jax.random.normal(own_key, dims, jnp.float32) * spread * gain
    return jnp.minimum(jnp.maximum(result, -limit), limit).astype(held_as)


def setup_inputs(seed: int = 0) -> dict:
    key_list = jax.random.split(jax.random.key(seed), 10)
    tokens = scatter_about(key_list[0], (TOKENS, MODEL_DIM), 1.0, 6.0, ((0, 32),))
    residual = scatter_about(key_list[1], (TOKENS, MODEL_DIM), 1.0, 6.0, ((0, 32),))
    token_adapter_index_keys = jax.random.split(jax.random.fold_in(key_list[2], 1), TOKENS // TOK_DEV)
    token_adapter_index_turns = jax.random.permutation(jax.random.fold_in(key_list[2], 3), TOKENS // TOK_DEV)
    token_adapter_index = jax.vmap(lambda own, number: routed_block(jax.random.fold_in(key_list[2], 2), own, number, TOK_DEV, ADAPTER_COUNT, 1, MOST, 2))(token_adapter_index_keys, token_adapter_index_turns).reshape((TOKENS, 1))
    adapter_down_weight = scatter_about(key_list[3], (ADAPTER_COUNT, ADAPTER_RANK, MODEL_DIM), MODEL_DIM ** -0.5, 0.0625, ((0, 8), (2, 4)))
    adapter_up_weight = scatter_about(key_list[4], (ADAPTER_COUNT, ADAPTER_RANK, MODEL_DIM), ADAPTER_RANK ** -0.5, 0.75, ((0, 8), (2, 4)))
    down_moment_first = scatter_about(key_list[5], (ADAPTER_COUNT, ADAPTER_RANK, MODEL_DIM), (1.2 * TENANT_ROWS ** 0.5), 135.0, ((0, 8), (2, 4)))
    down_moment_second = jnp.clip(jnp.exp(math.log(6144.0) - 3.4051113 * jax.random.uniform(key_list[6], (ADAPTER_COUNT, ADAPTER_RANK, MODEL_DIM), jnp.float32) ** level_of(key_list[6], (ADAPTER_COUNT, ADAPTER_RANK, MODEL_DIM), ((0, 8), (2, 4)), -0.2, 0.2)), 204.0, 6144.0).astype(jnp.bfloat16)
    up_moment_first = scatter_about(key_list[7], (ADAPTER_COUNT, ADAPTER_RANK, MODEL_DIM), (0.1 * TENANT_ROWS ** 0.5), 13.5625, ((0, 8), (2, 4)))
    up_moment_second = jnp.clip(jnp.exp(math.log(51.0) - 3.5057412 * jax.random.uniform(key_list[8], (ADAPTER_COUNT, ADAPTER_RANK, MODEL_DIM), jnp.float32) ** level_of(key_list[8], (ADAPTER_COUNT, ADAPTER_RANK, MODEL_DIM), ((0, 8), (2, 4)), -0.2, 0.2)), 1.53125, 51.0).astype(jnp.bfloat16)
    return dict(tokens=tokens, residual=residual, token_adapter_index=token_adapter_index, adapter_down_weight=adapter_down_weight, adapter_up_weight=adapter_up_weight, down_moment_first=down_moment_first, down_moment_second=down_moment_second, up_moment_first=up_moment_first, up_moment_second=up_moment_second)


adapter_scale = 0.5
adam_eps = 1e-08

def adam_update(grad, first, second):
    first_new = 0.9 * first.astype(jnp.float32) + 0.1 * grad
    second_new = 0.95 * second.astype(jnp.float32) + 0.05 * grad * grad
    return first_new / (jnp.sqrt(second_new) + adam_eps)

def reference(tokens, residual, token_adapter_index, adapter_down_weight, adapter_up_weight, down_moment_first, down_moment_second, up_moment_first, up_moment_second):
    route_ids = token_adapter_index[:, 0]
    slots = N_DP * N_OWNER * MOST

    def per_adapter(adapter_slot):
        positions = jnp.nonzero(route_ids == adapter_slot, size=slots, fill_value=TOKENS)[0].astype(jnp.int32)
        present = positions < TOKENS
        clipped = jnp.minimum(positions, TOKENS - 1)
        row_block = jnp.where(present[:, None], tokens[clipped], jnp.zeros((), tokens.dtype))
        residual_row_block = jnp.where(present[:, None], residual[clipped].astype(jnp.float32), jnp.zeros((), jnp.float32))
        down_row_block = adapter_down_weight[adapter_slot]
        up_row_block = adapter_up_weight[adapter_slot]
        hidden_state = lax.dot_general(row_block, down_row_block, (((1,), (1,)), ((), ())), preferred_element_type=jnp.float32).astype(jnp.bfloat16)
        adapter_output = (adapter_scale * jnp.dot(hidden_state, up_row_block, preferred_element_type=jnp.float32)).astype(jnp.bfloat16)
        shifted_index = residual_row_block + adapter_output.astype(jnp.float32)
        row_loss = lax.optimization_barrier(jnp.mean(0.5 * shifted_index * shifted_index, axis=1))
        output_gradient = shifted_index.astype(jnp.bfloat16)
        up_gradient = adapter_scale * lax.dot_general(hidden_state, output_gradient, (((0,), (0,)), ((), ())), preferred_element_type=jnp.float32)
        hidden_gradient = (adapter_scale * lax.dot_general(output_gradient, up_row_block, (((1,), (1,)), ((), ())), preferred_element_type=jnp.float32)).astype(jnp.bfloat16)
        down_grad = lax.dot_general(hidden_gradient, row_block, (((0,), (0,)), ((), ())), preferred_element_type=jnp.float32)
        return (down_grad, up_gradient, row_loss, positions)
    down_grad, up_gradient, row_loss, positions = lax.map(per_adapter, jnp.arange(ADAPTER_COUNT, dtype=jnp.int32))
    token_loss = jnp.zeros((TOKENS,), jnp.float32).at[positions.reshape(-1)].set(row_loss.reshape(-1), mode='drop')
    down_update = adam_update(down_grad, down_moment_first, down_moment_second)
    up_update = adam_update(up_gradient, up_moment_first, up_moment_second)
    return (down_update, up_update, token_loss)
```

```python
import functools

import jax
import jax.numpy as jnp
from jax import lax
from jax.experimental import pallas as pl
from jax.experimental.pallas import tpu as pltpu
from jax.sharding import PartitionSpec as P

adapter_scale = 0.5
adam_eps = 1e-08


def adam_update(grad, first, second):
    first_new = 0.9 * first.astype(jnp.float32) + 0.1 * grad
    second_new = 0.95 * second.astype(jnp.float32) + 0.05 * grad * grad
    return first_new / (jnp.sqrt(second_new) + adam_eps)


def plain_body(
    tokens,
    residual,
    token_adapter_index,
    adapter_down_weight,
    adapter_up_weight,
    down_moment_first,
    down_moment_second,
    up_moment_first,
    up_moment_second,
):
    owner_index = lax.axis_size("owner")
    tok_rows = tokens.shape[0]
    model_width_value = tokens.shape[1]
    column_span = adapter_down_weight.shape[2]
    slot_capacity = max(2, 3 * tok_rows // (2 * owner_index))
    route_ids = token_adapter_index[:, 0]
    member = (route_ids[:, None] == jnp.arange(owner_index, dtype=jnp.int32)[None, :]).astype(
        jnp.int32
    )
    earlier = jnp.tril(jnp.ones((tok_rows, tok_rows), jnp.bfloat16), -1)
    before = jnp.dot(
        earlier, member.astype(jnp.bfloat16), preferred_element_type=jnp.float32
    ).astype(jnp.int32)
    within = jnp.sum(before * member, axis=1)
    target = route_ids * slot_capacity + within
    dispatch = (
        jnp.arange(owner_index * slot_capacity, dtype=jnp.int32)[:, None] == target[None, :]
    ).astype(jnp.bfloat16)

    def placed_rows(row_block):
        return jnp.dot(dispatch, row_block, preferred_element_type=jnp.float32).astype(jnp.bfloat16)

    down_full, up_weight_whole = (
        lax.all_gather(adapter_down_weight, "dp", axis=2, tiled=True),
        lax.all_gather(adapter_up_weight, "dp", axis=2, tiled=True),
    )
    down_full = down_full[0]
    up_weight_whole = up_weight_whole[0]

    def spread(row_block):
        return placed_rows(row_block).reshape(owner_index, slot_capacity, model_width_value)

    arrived = lax.all_to_all(
        spread(tokens), "owner", split_axis=0, concat_axis=0, tiled=True
    ).reshape(owner_index * slot_capacity, model_width_value)
    hidden_state = lax.dot_general(
        arrived, down_full, (((1,), (1,)), ((), ())), preferred_element_type=jnp.float32
    ).astype(jnp.bfloat16)
    adapter_output = (
        adapter_scale * jnp.dot(hidden_state, up_weight_whole, preferred_element_type=jnp.float32)
    ).astype(jnp.bfloat16)
    hidden_state, adapter_output = (hidden_state, adapter_output)
    returned = lax.all_to_all(
        adapter_output.reshape(owner_index, slot_capacity, model_width_value),
        "owner",
        split_axis=0,
        concat_axis=0,
        tiled=True,
    )
    returned = returned.reshape(owner_index * slot_capacity, model_width_value)
    adapter_home_index = lax.dot_general(
        dispatch, returned, (((0,), (0,)), ((), ())), preferred_element_type=jnp.float32
    )
    shifted_index = residual.astype(jnp.float32) + adapter_home_index
    token_loss = jnp.mean(0.5 * shifted_index * shifted_index, axis=1)
    output_gradient = lax.all_to_all(
        spread(shifted_index.astype(jnp.bfloat16)), "owner", split_axis=0, concat_axis=0, tiled=True
    )
    output_gradient = output_gradient.reshape(owner_index * slot_capacity, model_width_value)
    up_gradient = adapter_scale * lax.dot_general(
        hidden_state, output_gradient, (((0,), (0,)), ((), ())), preferred_element_type=jnp.float32
    )
    hidden_gradient = (
        adapter_scale
        * lax.dot_general(
            output_gradient,
            up_weight_whole,
            (((1,), (1,)), ((), ())),
            preferred_element_type=jnp.float32,
        )
    ).astype(jnp.bfloat16)
    down_grad = lax.dot_general(
        hidden_gradient, arrived, (((0,), (0,)), ((), ())), preferred_element_type=jnp.float32
    )
    summed_down, summed_up = lax.psum((down_grad, up_gradient), "dp")
    offset = lax.axis_index("dp") * column_span
    down_share = lax.dynamic_slice_in_dim(summed_down, offset, column_span, 1)
    up_share = lax.dynamic_slice_in_dim(summed_up, offset, column_span, 1)
    down_update = adam_update(down_share, down_moment_first[0], down_moment_second[0])
    up_update = adam_update(up_share, up_moment_first[0], up_moment_second[0])
    return (down_update[None], up_update[None], token_loss)


MESH = pl.DeviceIdType.MESH
F32, BF16 = jnp.float32, jnp.bfloat16
FOLD = 2


def dot_rows(a, b):
    return lax.dot_general(a, b, (((1,), (1,)), ((), ())), preferred_element_type=F32)


def dot_sum(a, b):
    return lax.dot_general(a, b, (((0,), (0,)), ((), ())), preferred_element_type=F32)


def kernel(
    sizes,
    ids_ref,
    tok_ref,
    res_ref,
    down_ref,
    up_ref,
    down_first,
    down_second,
    up_first,
    up_second,
    down_out,
    up_out,
    loss_out,
    tok_placed,
    res_placed,
    tok_here,
    res_here,
    down_all,
    up_all,
    up_sum,
    down_sum,
    up_part,
    down_part,
    up_heard,
    down_heard,
    loss_part,
    loss_heard,
    tok_send,
    tok_recv,
    res_send,
    res_recv,
    weight_send,
    weight_recv,
    grad_send,
    grad_recv,
    loss_send,
    loss_recv,
    own_sem,
):
    n_dp, n_owner, cap, rank, parts = sizes
    slab = FOLD * cap
    rows = n_owner * slab
    toks, width = tok_ref.shape
    half = width // FOLD
    span = width // n_dp
    step = half // parts
    per = half // span
    d, o = lax.axis_index("dp"), lax.axis_index("owner")

    def flipped(k):
        peer, bit = 0, 1
        while bit < n_owner:
            own = (o // bit) % 2
            peer = peer + bit * ((own + (k // bit) % 2) % 2)
            bit *= 2
        return peer

    peers = [flipped(k) for k in range(1, n_owner)]
    others = [lax.rem(d + k, n_dp) for k in range(1, n_dp)]

    barrier = pltpu.get_barrier_semaphore()
    for p in peers:
        pl.semaphore_signal(barrier, inc=1, device_id=(d, p), device_id_type=MESH)
    for q in others:
        pl.semaphore_signal(barrier, inc=1, device_id=(q, o), device_id_type=MESH)

    ids = ids_ref[...]
    member = (lax.broadcasted_iota(jnp.int32, (n_owner, toks), 0) == ids).astype(F32)
    upper = (
        lax.broadcasted_iota(jnp.int32, (toks, toks), 0)
        < lax.broadcasted_iota(jnp.int32, (toks, toks), 1)
    ).astype(F32)
    before = jnp.dot(member.astype(BF16), upper.astype(BF16), preferred_element_type=F32)
    within = jnp.sum(before * member, axis=0, keepdims=True)
    target = ids.astype(F32) * float(slab) + within
    row = lax.broadcasted_iota(jnp.int32, (rows, toks), 0).astype(F32)
    first_half = (row == target).astype(F32)
    second_half = (row == target + float(cap)).astype(F32)
    home = first_half + second_half
    dispatch = jnp.concatenate([first_half.astype(BF16), second_half.astype(BF16)], axis=1)

    def place(src, dst, c):
        two = jnp.concatenate(
            [src[:, c * step : (c + 1) * step], src[:, half + c * step : half + (c + 1) * step]],
            axis=0,
        )
        dst[c] = jnp.dot(dispatch, two, preferred_element_type=F32).astype(BF16)

    mine = pl.ds(pl.multiple_of(o * slab, 16), slab)

    def to_owner(placed, here, send, recv, k, p, c):
        return pltpu.make_async_remote_copy(
            src_ref=placed.at[c, pl.ds(pl.multiple_of(p * slab, 16), slab)],
            dst_ref=here.at[c, mine],
            send_sem=send.at[k, c],
            recv_sem=recv.at[k, c],
            device_id=(d, p),
            device_id_type=MESH,
        )

    def slice_of(ref, q):
        return ref.at[
            pl.ds(pl.multiple_of((q // per) * rank, 16), rank),
            pl.ds(pl.multiple_of((q % per) * span, 128), span),
        ]

    def weight_to(w, src, dst, k, q):
        return pltpu.make_async_remote_copy(
            src_ref=src,
            dst_ref=slice_of(dst, d),
            send_sem=weight_send.at[w, k],
            recv_sem=weight_recv.at[w, d],
            device_id=(q, o),
            device_id_type=MESH,
        )

    own = [
        pltpu.make_async_copy(down_ref, slice_of(down_all, d), own_sem.at[0]),
        pltpu.make_async_copy(up_ref, slice_of(up_all, d), own_sem.at[1]),
    ]
    for copy in own:
        copy.start()
    own_tok = [
        pltpu.make_async_copy(tok_placed.at[c, mine], tok_here.at[c, mine], own_sem.at[2 + c])
        for c in range(parts)
    ]
    own_res = [
        pltpu.make_async_copy(
            res_placed.at[c, mine], res_here.at[c, mine], own_sem.at[2 + parts + c]
        )
        for c in range(parts)
    ]

    place(tok_ref, tok_placed, 0)
    pl.semaphore_wait(barrier, len(peers) + len(others))

    weights = [
        [weight_to(w, src, dst, k, q) for k, q in enumerate(others)]
        for w, (src, dst) in enumerate(((down_ref, down_all), (up_ref, up_all)))
    ]
    tok_copies = [
        [to_owner(tok_placed, tok_here, tok_send, tok_recv, k, p, c) for k, p in enumerate(peers)]
        for c in range(parts)
    ]
    res_copies = [
        [to_owner(res_placed, res_here, res_send, res_recv, k, p, c) for k, p in enumerate(peers)]
        for c in range(parts)
    ]
    for c in range(parts):
        if c:
            place(tok_ref, tok_placed, c)
        for copy in tok_copies[c]:
            copy.start()
        own_tok[c].start()
        if c == 0:
            for copy in weights[0]:
                copy.start()
    for copy in weights[1]:
        copy.start()
    for c in range(parts):
        place(res_ref, res_placed, c)
        for copy in res_copies[c]:
            copy.start()
        own_res[c].start()

    def weight_arrived(w, dst):
        for q in others:
            pltpu.make_async_remote_copy(
                src_ref=slice_of(dst, q),
                dst_ref=slice_of(dst, q),
                send_sem=weight_send.at[w, 0],
                recv_sem=weight_recv.at[w, q],
                device_id=(q, o),
                device_id_type=MESH,
            ).wait_recv()
        own[w].wait()

    cols = lambda c: slice(c * step, (c + 1) * step)
    fold_row = (lax.broadcasted_iota(jnp.int32, (rows, FOLD * rank), 0) % slab) // cap
    fold_lane = lax.broadcasted_iota(jnp.int32, (rows, FOLD * rank), 1) // rank
    same = (fold_row == fold_lane).astype(F32)

    def folded(total, scale):
        kept = total * same
        both = kept + pltpu.roll(kept, rank, 1)
        both = both.reshape(n_owner, FOLD, cap, FOLD * rank)
        whole = both[:, 0] + both[:, 1]
        whole = jnp.stack([whole, whole], axis=1).reshape(rows, FOLD * rank)
        return (scale * whole * same).astype(BF16)

    weight_arrived(0, down_all)
    total = jnp.zeros((rows, FOLD * rank), F32)
    for c in range(parts):
        for copy in tok_copies[c]:
            copy.wait_recv()
        own_tok[c].wait()
        total = total + dot_rows(tok_here[c], down_all[:, cols(c)])
    hidden = folded(total, 1.0)

    weight_arrived(1, up_all)

    def grad_to(w, part, heard, q):
        return pltpu.make_async_remote_copy(
            src_ref=slice_of(part, q),
            dst_ref=heard.at[d],
            send_sem=grad_send.at[w, q],
            recv_sem=grad_recv.at[w, d],
            device_id=(q, o),
            device_id_type=MESH,
        )

    def send_group(w, part, heard, g):
        for q in range(g, n_dp, per):

            @pl.when(d != q)
            def _():
                grad_to(w, part, heard, q).start()

    ahead = parts // per
    loss_part[...] = jnp.zeros((rows, 128), F32)
    total = jnp.zeros((rows, FOLD * rank), F32)
    for c in range(parts):
        for copy in res_copies[c]:
            copy.wait_recv()
        own_res[c].wait()
        up_c = up_all[:, cols(c)]
        added = (adapter_scale * jnp.dot(hidden, up_c, preferred_element_type=F32)).astype(BF16)
        shifted = res_here[c].astype(F32) + added.astype(F32)
        square = shifted * shifted
        lanes = square[:, :128]
        for j in range(1, step // 128):
            lanes = lanes + square[:, j * 128 : (j + 1) * 128]
        loss_part[...] += lanes
        cotangent = shifted.astype(BF16)
        total = total + dot_rows(cotangent, up_c)
        up_c_grad = adapter_scale * dot_sum(hidden, cotangent)
        up_sum[:, cols(c)] = up_c_grad
        up_part[:, cols(c)] = up_c_grad.astype(BF16)
        if (c + 1) % ahead == 0:
            send_group(0, up_part, up_heard, c // ahead)
    hidden_grad = folded(total, adapter_scale)

    for c in range(parts):
        down_c_grad = dot_sum(hidden_grad, tok_here[c])
        down_sum[:, cols(c)] = down_c_grad
        down_part[:, cols(c)] = down_c_grad.astype(BF16)
        if (c + 1) % ahead == 0:
            send_group(1, down_part, down_heard, c // ahead)

    def loss_to(k, p):
        return pltpu.make_async_remote_copy(
            src_ref=loss_part.at[pl.ds(pl.multiple_of(p * slab, 8), slab)],
            dst_ref=loss_heard.at[mine],
            send_sem=loss_send.at[k],
            recv_sem=loss_recv.at[k],
            device_id=(d, p),
            device_id_type=MESH,
        )

    loss_copies = [loss_to(k, p) for k, p in enumerate(peers)]
    for copy in loss_copies:
        copy.start()
    loss_heard[mine, :] = loss_part[mine, :]

    def finish(w, part, heard, summed, first, second, out):
        for q in others:
            pltpu.make_async_remote_copy(
                src_ref=heard.at[q],
                dst_ref=heard.at[q],
                send_sem=grad_send.at[w, q],
                recv_sem=grad_recv.at[w, q],
                device_id=(q, o),
                device_id_type=MESH,
            ).wait_recv()
        grad = slice_of(summed, d)[...]
        for q in others:
            grad = grad + heard[q].astype(F32)
        out[...] = adam_update(grad, first[...], second[...])

    finish(0, up_part, up_heard, up_sum, up_first, up_second, up_out)

    for copy in loss_copies:
        copy.wait_recv()
    sums = jnp.sum(loss_heard[...], axis=1, keepdims=True)
    loss_out[...] = (0.5 / width) * jnp.sum(home * sums, axis=0, keepdims=True)

    finish(1, down_part, down_heard, down_sum, down_first, down_second, down_out)

    for group in weights + tok_copies + res_copies + [loss_copies]:
        for copy in group:
            copy.wait_send()
    for w, part, heard in ((0, up_part, up_heard), (1, down_part, down_heard)):
        for q in others:
            grad_to(w, part, heard, q).wait_send()


def kernel_body(
    n_dp,
    n_owner,
    cap,
    tokens,
    residual,
    token_adapter_index,
    adapter_down_weight,
    adapter_up_weight,
    down_moment_first,
    down_moment_second,
    up_moment_first,
    up_moment_second,
):
    toks, width = tokens.shape
    _, rank, span = adapter_down_weight.shape
    half, parts = width // FOLD, 4
    step = half // parts
    slab = FOLD * cap
    rows = n_owner * slab
    dma = pltpu.SemaphoreType.DMA
    down_update, up_update, token_loss = pl.pallas_call(
        functools.partial(kernel, (n_dp, n_owner, cap, rank, parts)),
        out_shape=(
            jax.ShapeDtypeStruct((rank, span), F32),
            jax.ShapeDtypeStruct((rank, span), F32),
            jax.ShapeDtypeStruct((1, toks), F32),
        ),
        in_specs=[pl.BlockSpec(memory_space=pltpu.VMEM)] * 9,
        out_specs=[pl.BlockSpec(memory_space=pltpu.VMEM)] * 3,
        scratch_shapes=[
            pltpu.VMEM((parts, rows, step), BF16),
            pltpu.VMEM((parts, rows, step), BF16),
            pltpu.VMEM((parts, rows, step), BF16),
            pltpu.VMEM((parts, rows, step), BF16),
            pltpu.VMEM((FOLD * rank, half), BF16),
            pltpu.VMEM((FOLD * rank, half), BF16),
            pltpu.VMEM((FOLD * rank, half), F32),
            pltpu.VMEM((FOLD * rank, half), F32),
            pltpu.VMEM((FOLD * rank, half), BF16),
            pltpu.VMEM((FOLD * rank, half), BF16),
            pltpu.VMEM((n_dp, rank, span), BF16),
            pltpu.VMEM((n_dp, rank, span), BF16),
            pltpu.VMEM((rows, 128), F32),
            pltpu.VMEM((rows, 128), F32),
            dma((n_owner - 1, parts)),
            dma((n_owner - 1, parts)),
            dma((n_owner - 1, parts)),
            dma((n_owner - 1, parts)),
            dma((2, n_dp)),
            dma((2, n_dp)),
            dma((2, n_dp)),
            dma((2, n_dp)),
            dma((n_owner - 1,)),
            dma((n_owner - 1,)),
            dma((2 + 2 * parts,)),
        ],
        compiler_params=pltpu.CompilerParams(
            collective_id=0, has_side_effects=True, vmem_limit_bytes=52 * 2**20
        ),
        name="step",
    )(
        token_adapter_index.reshape(1, toks),
        tokens,
        residual,
        adapter_down_weight[0],
        adapter_up_weight[0],
        down_moment_first[0],
        down_moment_second[0],
        up_moment_first[0],
        up_moment_second[0],
    )
    return (down_update[None], up_update[None], token_loss[0])


def solution(mesh):
    n_dp, n_owner = mesh.shape["dp"], mesh.shape["owner"]

    def body(*arrays):
        toks = arrays[0].shape[0]
        cap = max(2, 3 * toks // (2 * n_owner))
        if cap % 8 == 0 and FOLD * cap % 16 == 0 and n_dp % FOLD == 0 and FOLD * 2 == n_dp:
            return kernel_body(n_dp, n_owner, cap, *arrays)
        return plain_body(*arrays)

    return jax.shard_map(
        body,
        mesh=mesh,
        in_specs=(
            P(("dp", "owner"), None),
            P(("dp", "owner"), None),
            P(("dp", "owner"), None),
            P("owner", None, "dp"),
            P("owner", None, "dp"),
            P("owner", None, "dp"),
            P("owner", None, "dp"),
            P("owner", None, "dp"),
            P("owner", None, "dp"),
        ),
        out_specs=(P("owner", None, "dp"), P("owner", None, "dp"), P(("dp", "owner"))),
        check_vma=False,
    )
```

```python
import functools

import jax
import jax.numpy as jnp
from jax import lax
from jax.experimental import pallas as pl
from jax.experimental.pallas import tpu as pltpu
from jax.sharding import PartitionSpec as P

adapter_scale = 0.5
adam_eps = 1e-08


def adam_update(grad, first, second):
    first_new = 0.9 * first.astype(jnp.float32) + 0.1 * grad
    second_new = 0.95 * second.astype(jnp.float32) + 0.05 * grad * grad
    return first_new / (jnp.sqrt(second_new) + adam_eps)


def plain_body(
    tokens,
    residual,
    token_adapter_index,
    adapter_down_weight,
    adapter_up_weight,
    down_moment_first,
    down_moment_second,
    up_moment_first,
    up_moment_second,
):
    owner_index = lax.axis_size("owner")
    tok_rows = tokens.shape[0]
    model_width_value = tokens.shape[1]
    column_span = adapter_down_weight.shape[2]
    slot_capacity = max(2, 3 * tok_rows // (2 * owner_index))
    route_ids = token_adapter_index[:, 0]
    member = (route_ids[:, None] == jnp.arange(owner_index, dtype=jnp.int32)[None, :]).astype(
        jnp.int32
    )
    earlier = jnp.tril(jnp.ones((tok_rows, tok_rows), jnp.bfloat16), -1)
    before = jnp.dot(
        earlier, member.astype(jnp.bfloat16), preferred_element_type=jnp.float32
    ).astype(jnp.int32)
    within = jnp.sum(before * member, axis=1)
    target = route_ids * slot_capacity + within
    dispatch = (
        jnp.arange(owner_index * slot_capacity, dtype=jnp.int32)[:, None] == target[None, :]
    ).astype(jnp.bfloat16)

    def placed_rows(row_block):
        return jnp.dot(dispatch, row_block, preferred_element_type=jnp.float32).astype(jnp.bfloat16)

    down_full, up_weight_whole = (
        lax.all_gather(adapter_down_weight, "dp", axis=2, tiled=True),
        lax.all_gather(adapter_up_weight, "dp", axis=2, tiled=True),
    )
    down_full = down_full[0]
    up_weight_whole = up_weight_whole[0]

    def spread(row_block):
        return placed_rows(row_block).reshape(owner_index, slot_capacity, model_width_value)

    arrived = lax.all_to_all(
        spread(tokens), "owner", split_axis=0, concat_axis=0, tiled=True
    ).reshape(owner_index * slot_capacity, model_width_value)
    hidden_state = lax.dot_general(
        arrived, down_full, (((1,), (1,)), ((), ())), preferred_element_type=jnp.float32
    ).astype(jnp.bfloat16)
    adapter_output = (
        adapter_scale * jnp.dot(hidden_state, up_weight_whole, preferred_element_type=jnp.float32)
    ).astype(jnp.bfloat16)
    hidden_state, adapter_output = (hidden_state, adapter_output)
    returned = lax.all_to_all(
        adapter_output.reshape(owner_index, slot_capacity, model_width_value),
        "owner",
        split_axis=0,
        concat_axis=0,
        tiled=True,
    )
    returned = returned.reshape(owner_index * slot_capacity, model_width_value)
    adapter_home_index = lax.dot_general(
        dispatch, returned, (((0,), (0,)), ((), ())), preferred_element_type=jnp.float32
    )
    shifted_index = residual.astype(jnp.float32) + adapter_home_index
    token_loss = jnp.mean(0.5 * shifted_index * shifted_index, axis=1)
    output_gradient = lax.all_to_all(
        spread(shifted_index.astype(jnp.bfloat16)), "owner", split_axis=0, concat_axis=0, tiled=True
    )
    output_gradient = output_gradient.reshape(owner_index * slot_capacity, model_width_value)
    up_gradient = adapter_scale * lax.dot_general(
        hidden_state, output_gradient, (((0,), (0,)), ((), ())), preferred_element_type=jnp.float32
    )
    hidden_gradient = (
        adapter_scale
        * lax.dot_general(
            output_gradient,
            up_weight_whole,
            (((1,), (1,)), ((), ())),
            preferred_element_type=jnp.float32,
        )
    ).astype(jnp.bfloat16)
    down_grad = lax.dot_general(
        hidden_gradient, arrived, (((0,), (0,)), ((), ())), preferred_element_type=jnp.float32
    )
    summed_down, summed_up = lax.psum((down_grad, up_gradient), "dp")
    offset = lax.axis_index("dp") * column_span
    down_share = lax.dynamic_slice_in_dim(summed_down, offset, column_span, 1)
    up_share = lax.dynamic_slice_in_dim(summed_up, offset, column_span, 1)
    down_update = adam_update(down_share, down_moment_first[0], down_moment_second[0])
    up_update = adam_update(up_share, up_moment_first[0], up_moment_second[0])
    return (down_update[None], up_update[None], token_loss)


MESH = pl.DeviceIdType.MESH
F32, BF16 = jnp.float32, jnp.bfloat16
FOLD = 2


def dot_rows(a, b):
    return lax.dot_general(a, b, (((1,), (1,)), ((), ())), preferred_element_type=F32)


def dot_sum(a, b):
    return lax.dot_general(a, b, (((0,), (0,)), ((), ())), preferred_element_type=F32)


def kernel(
    sizes,
    ids_ref,
    tok_ref,
    res_ref,
    down_ref,
    up_ref,
    down_out,
    up_out,
    loss_out,
    tok_in,
    res_in,
    tok_placed,
    res_placed,
    tok_here,
    res_here,
    down_all,
    up_all,
    up_sum,
    down_sum,
    up_part,
    down_part,
    up_heard,
    down_heard,
    loss_part,
    loss_heard,
    tok_send,
    tok_recv,
    res_send,
    res_recv,
    weight_send,
    weight_recv,
    grad_send,
    grad_recv,
    loss_send,
    loss_recv,
    own_sem,
    in_sem,
):
    n_dp, n_owner, cap, rank, parts = sizes
    slab = FOLD * cap
    rows = n_owner * slab
    toks, width = tok_ref.shape
    half = width // FOLD
    span = width // n_dp
    step = half // parts
    per = half // span
    d, o = lax.axis_index("dp"), lax.axis_index("owner")

    def flipped(k):
        peer, bit = 0, 1
        while bit < n_owner:
            own = (o // bit) % 2
            peer = peer + bit * ((own + (k // bit) % 2) % 2)
            bit *= 2
        return peer

    near = sorted(range(1, n_owner), key=lambda k: (k % 2, -k))
    peers = [flipped(k) for k in near]
    others = [lax.rem(d + k, n_dp) for k in range(1, n_dp)]

    def slice_of(ref, q):
        return ref.at[
            pl.ds(pl.multiple_of((q // per) * rank, 16), rank),
            pl.ds(pl.multiple_of((q % per) * span, 128), span),
        ]

    barrier = pltpu.get_barrier_semaphore()
    for p in peers:
        pl.semaphore_signal(barrier, inc=1, device_id=(d, p), device_id_type=MESH)
    for q in others:
        pl.semaphore_signal(barrier, inc=1, device_id=(q, o), device_id_type=MESH)

    loads = [
        pltpu.make_async_copy(src, dst, in_sem.at[i])
        for i, (src, dst) in enumerate(
            (
                (down_ref, slice_of(down_all, d)),
                (tok_ref, tok_in),
                (up_ref, slice_of(up_all, d)),
                (res_ref, res_in),
            )
        )
    ]
    for load in loads:
        load.start()

    ids = ids_ref[...]
    member = (lax.broadcasted_iota(jnp.int32, (n_owner, toks), 0) == ids).astype(F32)
    upper = (
        lax.broadcasted_iota(jnp.int32, (toks, toks), 0)
        < lax.broadcasted_iota(jnp.int32, (toks, toks), 1)
    ).astype(F32)
    before = jnp.dot(member.astype(BF16), upper.astype(BF16), preferred_element_type=F32)
    within = jnp.sum(before * member, axis=0, keepdims=True)
    target = ids.astype(F32) * float(slab) + within
    row = lax.broadcasted_iota(jnp.int32, (rows, toks), 0).astype(F32)
    first_half = (row == target).astype(F32)
    second_half = (row == target + float(cap)).astype(F32)
    home = first_half + second_half
    dispatch = jnp.concatenate([first_half.astype(BF16), second_half.astype(BF16)], axis=1)

    def place(src, dst, c):
        two = jnp.concatenate(
            [src[:, c * step : (c + 1) * step], src[:, half + c * step : half + (c + 1) * step]],
            axis=0,
        )
        dst[c] = jnp.dot(dispatch, two, preferred_element_type=F32).astype(BF16)

    mine = pl.ds(pl.multiple_of(o * slab, 16), slab)

    def to_owner(placed, here, send, recv, k, p, c):
        return pltpu.make_async_remote_copy(
            src_ref=placed.at[c, pl.ds(pl.multiple_of(p * slab, 16), slab)],
            dst_ref=here.at[c, mine],
            send_sem=send.at[k, c],
            recv_sem=recv.at[k, c],
            device_id=(d, p),
            device_id_type=MESH,
        )

    def weight_to(w, dst, k, q):
        return pltpu.make_async_remote_copy(
            src_ref=slice_of(dst, d),
            dst_ref=slice_of(dst, d),
            send_sem=weight_send.at[w, k],
            recv_sem=weight_recv.at[w, d],
            device_id=(q, o),
            device_id_type=MESH,
        )

    own_tok = [
        pltpu.make_async_copy(tok_placed.at[c, mine], tok_here.at[c, mine], own_sem.at[c])
        for c in range(parts)
    ]
    own_res = [
        pltpu.make_async_copy(
            res_placed.at[c, mine], res_here.at[c, mine], own_sem.at[parts + c]
        )
        for c in range(parts)
    ]

    weights = [
        [weight_to(w, dst, k, q) for k, q in enumerate(others)]
        for w, dst in enumerate((down_all, up_all))
    ]
    tok_copies = [
        [to_owner(tok_placed, tok_here, tok_send, tok_recv, k, p, c) for k, p in enumerate(peers)]
        for c in range(parts)
    ]
    res_copies = [
        [to_owner(res_placed, res_here, res_send, res_recv, k, p, c) for k, p in enumerate(peers)]
        for c in range(parts)
    ]
    loads[1].wait()
    place(tok_in, tok_placed, 0)
    loads[0].wait()
    pl.semaphore_wait(barrier, len(peers) + len(others))
    for copy in weights[0]:
        copy.start()
    for c in range(parts):
        if c:
            place(tok_in, tok_placed, c)
        for copy in tok_copies[c]:
            copy.start()
        own_tok[c].start()
    loads[2].wait()
    for copy in weights[1]:
        copy.start()
    loads[3].wait()
    for c in range(parts):
        place(res_in, res_placed, c)
        for copy in res_copies[c]:
            copy.start()
        own_res[c].start()

    def weight_arrived(w, dst):
        for q in others:
            pltpu.make_async_remote_copy(
                src_ref=slice_of(dst, q),
                dst_ref=slice_of(dst, q),
                send_sem=weight_send.at[w, 0],
                recv_sem=weight_recv.at[w, q],
                device_id=(q, o),
                device_id_type=MESH,
            ).wait_recv()

    cols = lambda c: slice(c * step, (c + 1) * step)
    fold_row = (lax.broadcasted_iota(jnp.int32, (rows, FOLD * rank), 0) % slab) // cap
    fold_lane = lax.broadcasted_iota(jnp.int32, (rows, FOLD * rank), 1) // rank
    same = (fold_row == fold_lane).astype(F32)

    def folded(total, scale):
        kept = total * same
        both = kept + pltpu.roll(kept, rank, 1)
        both = both.reshape(n_owner, FOLD, cap, FOLD * rank)
        whole = both[:, 0] + both[:, 1]
        whole = jnp.stack([whole, whole], axis=1).reshape(rows, FOLD * rank)
        return (scale * whole * same).astype(BF16)

    weight_arrived(0, down_all)
    total = jnp.zeros((rows, FOLD * rank), F32)
    for c in range(parts):
        for copy in tok_copies[c]:
            copy.wait_recv()
        own_tok[c].wait()
        total = total + dot_rows(tok_here[c], down_all[:, cols(c)])
    hidden = folded(total, 1.0)

    weight_arrived(1, up_all)

    ahead = parts // per

    def grad_to(w, part, heard, q, j):
        return pltpu.make_async_remote_copy(
            src_ref=part.at[
                pl.ds(pl.multiple_of((q // per) * rank, 16), rank),
                pl.ds(pl.multiple_of((q % per) * span + j * step, 128), step),
            ],
            dst_ref=heard.at[d, j],
            send_sem=grad_send.at[w, q, j],
            recv_sem=grad_recv.at[w, d, j],
            device_id=(q, o),
            device_id_type=MESH,
        )

    def send_piece(w, part, heard, c):
        for q in range(c // ahead, n_dp, per):

            @pl.when(d != q)
            def _():
                grad_to(w, part, heard, q, c % ahead).start()

    loss_part[...] = jnp.zeros((rows, 128), F32)
    total = jnp.zeros((rows, FOLD * rank), F32)
    for c in range(parts):
        for copy in res_copies[c]:
            copy.wait_recv()
        own_res[c].wait()
        up_c = up_all[:, cols(c)]
        added = (adapter_scale * jnp.dot(hidden, up_c, preferred_element_type=F32)).astype(BF16)
        shifted = res_here[c].astype(F32) + added.astype(F32)
        square = shifted * shifted
        lanes = square[:, :128]
        for j in range(1, step // 128):
            lanes = lanes + square[:, j * 128 : (j + 1) * 128]
        loss_part[...] += lanes
        cotangent = shifted.astype(BF16)
        total = total + dot_rows(cotangent, up_c)
        up_c_grad = adapter_scale * dot_sum(hidden, cotangent)
        up_sum[:, cols(c)] = up_c_grad
        up_part[:, cols(c)] = up_c_grad.astype(BF16)
        send_piece(0, up_part, up_heard, c)
    hidden_grad = folded(total, adapter_scale)

    for c in range(parts):
        down_c_grad = dot_sum(hidden_grad, tok_here[c])
        down_sum[:, cols(c)] = down_c_grad
        down_part[:, cols(c)] = down_c_grad.astype(BF16)
        send_piece(1, down_part, down_heard, c)

    def loss_to(k, p):
        return pltpu.make_async_remote_copy(
            src_ref=loss_part.at[pl.ds(pl.multiple_of(p * slab, 8), slab)],
            dst_ref=loss_heard.at[mine],
            send_sem=loss_send.at[k],
            recv_sem=loss_recv.at[k],
            device_id=(d, p),
            device_id_type=MESH,
        )

    loss_copies = [loss_to(k, p) for k, p in enumerate(peers)]
    for copy in loss_copies:
        copy.start()
    loss_heard[mine, :] = loss_part[mine, :]

    def finish(w, heard, summed, out):
        for j in range(ahead):
            for q in others:
                pltpu.make_async_remote_copy(
                    src_ref=heard.at[q, j],
                    dst_ref=heard.at[q, j],
                    send_sem=grad_send.at[w, q, j],
                    recv_sem=grad_recv.at[w, q, j],
                    device_id=(q, o),
                    device_id_type=MESH,
                ).wait_recv()
            grad = summed[
                pl.ds(pl.multiple_of((d // per) * rank, 16), rank),
                pl.ds(pl.multiple_of((d % per) * span + j * step, 128), step),
            ]
            for q in others:
                grad = grad + heard[q, j].astype(F32)
            out[:, j * step : (j + 1) * step] = grad

    finish(0, up_heard, up_sum, up_out)

    for copy in loss_copies:
        copy.wait_recv()
    sums = jnp.sum(loss_heard[...], axis=1, keepdims=True)
    loss_out[...] = jnp.sum(home * sums, axis=0, keepdims=True)

    finish(1, down_heard, down_sum, down_out)

    for group in weights + tok_copies + res_copies + [loss_copies]:
        for copy in group:
            copy.wait_send()
    for w, part, heard in ((0, up_part, up_heard), (1, down_part, down_heard)):
        for q in others:
            for j in range(ahead):
                grad_to(w, part, heard, q, j).wait_send()


def kernel_body(
    n_dp,
    n_owner,
    cap,
    tokens,
    residual,
    token_adapter_index,
    adapter_down_weight,
    adapter_up_weight,
    down_moment_first,
    down_moment_second,
    up_moment_first,
    up_moment_second,
):
    toks, width = tokens.shape
    _, rank, span = adapter_down_weight.shape
    half, parts = width // FOLD, 4
    step = half // parts
    pieces = span // step
    slab = FOLD * cap
    rows = n_owner * slab
    dma = pltpu.SemaphoreType.DMA
    down_grad, up_grad, row_loss = pl.pallas_call(
        functools.partial(kernel, (n_dp, n_owner, cap, rank, parts)),
        out_shape=(
            jax.ShapeDtypeStruct((rank, span), F32),
            jax.ShapeDtypeStruct((rank, span), F32),
            jax.ShapeDtypeStruct((1, toks), F32),
        ),
        in_specs=[pl.BlockSpec(memory_space=pltpu.VMEM)]
        + [pl.BlockSpec(memory_space=pltpu.HBM)] * 4,
        out_specs=[pl.BlockSpec(memory_space=pltpu.VMEM)] * 3,
        scratch_shapes=[
            pltpu.VMEM((toks, width), BF16),
            pltpu.VMEM((toks, width), BF16),
            pltpu.VMEM((parts, rows, step), BF16),
            pltpu.VMEM((parts, rows, step), BF16),
            pltpu.VMEM((parts, rows, step), BF16),
            pltpu.VMEM((parts, rows, step), BF16),
            pltpu.VMEM((FOLD * rank, half), BF16),
            pltpu.VMEM((FOLD * rank, half), BF16),
            pltpu.VMEM((FOLD * rank, half), F32),
            pltpu.VMEM((FOLD * rank, half), F32),
            pltpu.VMEM((FOLD * rank, half), BF16),
            pltpu.VMEM((FOLD * rank, half), BF16),
            pltpu.VMEM((n_dp, pieces, rank, step), BF16),
            pltpu.VMEM((n_dp, pieces, rank, step), BF16),
            pltpu.VMEM((rows, 128), F32),
            pltpu.VMEM((rows, 128), F32),
            dma((n_owner - 1, parts)),
            dma((n_owner - 1, parts)),
            dma((n_owner - 1, parts)),
            dma((n_owner - 1, parts)),
            dma((2, n_dp)),
            dma((2, n_dp)),
            dma((2, n_dp, pieces)),
            dma((2, n_dp, pieces)),
            dma((n_owner - 1,)),
            dma((n_owner - 1,)),
            dma((2 * parts,)),
            dma((4,)),
        ],
        compiler_params=pltpu.CompilerParams(
            collective_id=0, has_side_effects=True, vmem_limit_bytes=52 * 2**20
        ),
        name="step",
    )(
        token_adapter_index.reshape(1, toks),
        tokens,
        residual,
        adapter_down_weight[0],
        adapter_up_weight[0],
    )
    down_update = adam_update(down_grad[None], down_moment_first, down_moment_second)
    up_update = adam_update(up_grad[None], up_moment_first, up_moment_second)
    return (down_update, up_update, (0.5 / width) * row_loss[0])


def solution(mesh):
    n_dp, n_owner = mesh.shape["dp"], mesh.shape["owner"]

    def body(*arrays):
        toks = arrays[0].shape[0]
        cap = max(2, 3 * toks // (2 * n_owner))
        if cap % 8 == 0 and FOLD * cap % 16 == 0 and n_dp % FOLD == 0 and FOLD * 2 == n_dp:
            return kernel_body(n_dp, n_owner, cap, *arrays)
        return plain_body(*arrays)

    return jax.shard_map(
        body,
        mesh=mesh,
        in_specs=(
            P(("dp", "owner"), None),
            P(("dp", "owner"), None),
            P(("dp", "owner"), None),
            P("owner", None, "dp"),
            P("owner", None, "dp"),
            P("owner", None, "dp"),
            P("owner", None, "dp"),
            P("owner", None, "dp"),
            P("owner", None, "dp"),
        ),
        out_specs=(P("owner", None, "dp"), P("owner", None, "dp"), P(("dp", "owner"))),
        check_vma=False,
    )
```

```python
import functools

import jax
import jax.numpy as jnp
from jax import lax
from jax.experimental import pallas as pl
from jax.experimental.pallas import tpu as pltpu
from jax.sharding import PartitionSpec as P

adapter_scale = 0.5
adam_eps = 1e-08


def adam_update(grad, first, second):
    first_new = 0.9 * first.astype(jnp.float32) + 0.1 * grad
    second_new = 0.95 * second.astype(jnp.float32) + 0.05 * grad * grad
    return first_new / (jnp.sqrt(second_new) + adam_eps)


def plain_body(
    tokens,
    residual,
    token_adapter_index,
    adapter_down_weight,
    adapter_up_weight,
    down_moment_first,
    down_moment_second,
    up_moment_first,
    up_moment_second,
):
    owner_index = lax.axis_size("owner")
    tok_rows = tokens.shape[0]
    model_width_value = tokens.shape[1]
    column_span = adapter_down_weight.shape[2]
    slot_capacity = max(2, 3 * tok_rows // (2 * owner_index))
    route_ids = token_adapter_index[:, 0]
    member = (route_ids[:, None] == jnp.arange(owner_index, dtype=jnp.int32)[None, :]).astype(
        jnp.int32
    )
    earlier = jnp.tril(jnp.ones((tok_rows, tok_rows), jnp.bfloat16), -1)
    before = jnp.dot(
        earlier, member.astype(jnp.bfloat16), preferred_element_type=jnp.float32
    ).astype(jnp.int32)
    within = jnp.sum(before * member, axis=1)
    target = route_ids * slot_capacity + within
    dispatch = (
        jnp.arange(owner_index * slot_capacity, dtype=jnp.int32)[:, None] == target[None, :]
    ).astype(jnp.bfloat16)

    def placed_rows(row_block):
        return jnp.dot(dispatch, row_block, preferred_element_type=jnp.float32).astype(jnp.bfloat16)

    down_full, up_weight_whole = (
        lax.all_gather(adapter_down_weight, "dp", axis=2, tiled=True),
        lax.all_gather(adapter_up_weight, "dp", axis=2, tiled=True),
    )
    down_full = down_full[0]
    up_weight_whole = up_weight_whole[0]

    def spread(row_block):
        return placed_rows(row_block).reshape(owner_index, slot_capacity, model_width_value)

    arrived = lax.all_to_all(
        spread(tokens), "owner", split_axis=0, concat_axis=0, tiled=True
    ).reshape(owner_index * slot_capacity, model_width_value)
    hidden_state = lax.dot_general(
        arrived, down_full, (((1,), (1,)), ((), ())), preferred_element_type=jnp.float32
    ).astype(jnp.bfloat16)
    adapter_output = (
        adapter_scale * jnp.dot(hidden_state, up_weight_whole, preferred_element_type=jnp.float32)
    ).astype(jnp.bfloat16)
    hidden_state, adapter_output = (hidden_state, adapter_output)
    returned = lax.all_to_all(
        adapter_output.reshape(owner_index, slot_capacity, model_width_value),
        "owner",
        split_axis=0,
        concat_axis=0,
        tiled=True,
    )
    returned = returned.reshape(owner_index * slot_capacity, model_width_value)
    adapter_home_index = lax.dot_general(
        dispatch, returned, (((0,), (0,)), ((), ())), preferred_element_type=jnp.float32
    )
    shifted_index = residual.astype(jnp.float32) + adapter_home_index
    token_loss = jnp.mean(0.5 * shifted_index * shifted_index, axis=1)
    output_gradient = lax.all_to_all(
        spread(shifted_index.astype(jnp.bfloat16)), "owner", split_axis=0, concat_axis=0, tiled=True
    )
    output_gradient = output_gradient.reshape(owner_index * slot_capacity, model_width_value)
    up_gradient = adapter_scale * lax.dot_general(
        hidden_state, output_gradient, (((0,), (0,)), ((), ())), preferred_element_type=jnp.float32
    )
    hidden_gradient = (
        adapter_scale
        * lax.dot_general(
            output_gradient,
            up_weight_whole,
            (((1,), (1,)), ((), ())),
            preferred_element_type=jnp.float32,
        )
    ).astype(jnp.bfloat16)
    down_grad = lax.dot_general(
        hidden_gradient, arrived, (((0,), (0,)), ((), ())), preferred_element_type=jnp.float32
    )
    summed_down, summed_up = lax.psum((down_grad, up_gradient), "dp")
    offset = lax.axis_index("dp") * column_span
    down_share = lax.dynamic_slice_in_dim(summed_down, offset, column_span, 1)
    up_share = lax.dynamic_slice_in_dim(summed_up, offset, column_span, 1)
    down_update = adam_update(down_share, down_moment_first[0], down_moment_second[0])
    up_update = adam_update(up_share, up_moment_first[0], up_moment_second[0])
    return (down_update[None], up_update[None], token_loss)


MESH = pl.DeviceIdType.MESH
F32, BF16 = jnp.float32, jnp.bfloat16
FOLD = 2


def dot_rows(a, b):
    return lax.dot_general(a, b, (((1,), (1,)), ((), ())), preferred_element_type=F32)


def dot_sum(a, b):
    return lax.dot_general(a, b, (((0,), (0,)), ((), ())), preferred_element_type=F32)


def kernel(
    sizes,
    ids_ref,
    tok_ref,
    res_ref,
    down_ref,
    up_ref,
    down_out,
    up_out,
    loss_out,
    tok_in,
    res_in,
    tok_placed,
    res_placed,
    tok_here,
    res_here,
    down_all,
    up_all,
    up_sum,
    down_sum,
    up_part,
    down_part,
    up_heard,
    down_heard,
    loss_part,
    loss_heard,
    tok_send,
    tok_recv,
    res_send,
    res_recv,
    weight_send,
    weight_recv,
    grad_send,
    grad_recv,
    loss_send,
    loss_recv,
    own_sem,
    in_sem,
):
    n_dp, n_owner, cap, rank, parts = sizes
    slab = FOLD * cap
    rows = n_owner * slab
    toks, width = tok_ref.shape
    half = width // FOLD
    span = width // n_dp
    step = half // parts
    per = half // span
    d, o = lax.axis_index("dp"), lax.axis_index("owner")

    def flipped(k):
        peer, bit = 0, 1
        while bit < n_owner:
            own = (o // bit) % 2
            peer = peer + bit * ((own + (k // bit) % 2) % 2)
            bit *= 2
        return peer

    near = sorted(range(1, n_owner), key=lambda k: (k % 2, -k))
    peers = [flipped(k) for k in near]
    others = [lax.rem(d + k, n_dp) for k in range(1, n_dp)]

    def slice_of(ref, q):
        return ref.at[
            pl.ds(pl.multiple_of((q // per) * rank, 16), rank),
            pl.ds(pl.multiple_of((q % per) * span, 128), span),
        ]

    barrier = pltpu.get_barrier_semaphore()
    for p in peers:
        pl.semaphore_signal(barrier, inc=1, device_id=(d, p), device_id_type=MESH)
    for q in others:
        pl.semaphore_signal(barrier, inc=1, device_id=(q, o), device_id_type=MESH)

    loads = [
        pltpu.make_async_copy(src, dst, in_sem.at[i])
        for i, (src, dst) in enumerate(
            (
                (down_ref, slice_of(down_all, d)),
                (tok_ref, tok_in),
                (up_ref, slice_of(up_all, d)),
                (res_ref, res_in),
            )
        )
    ]
    for load in loads:
        load.start()

    ids = ids_ref[...]
    member = (lax.broadcasted_iota(jnp.int32, (n_owner, toks), 0) == ids).astype(F32)
    upper = (
        lax.broadcasted_iota(jnp.int32, (toks, toks), 0)
        < lax.broadcasted_iota(jnp.int32, (toks, toks), 1)
    ).astype(F32)
    before = jnp.dot(member.astype(BF16), upper.astype(BF16), preferred_element_type=F32)
    within = jnp.sum(before * member, axis=0, keepdims=True)
    target = ids.astype(F32) * float(slab) + within
    row = lax.broadcasted_iota(jnp.int32, (rows, toks), 0).astype(F32)
    first_half = (row == target).astype(F32)
    second_half = (row == target + float(cap)).astype(F32)
    home = first_half + second_half
    dispatch = jnp.concatenate([first_half.astype(BF16), second_half.astype(BF16)], axis=1)

    def place(src, dst, c):
        two = jnp.concatenate(
            [src[:, c * step : (c + 1) * step], src[:, half + c * step : half + (c + 1) * step]],
            axis=0,
        )
        dst[c] = jnp.dot(dispatch, two, preferred_element_type=F32).astype(BF16)

    mine = pl.ds(pl.multiple_of(o * slab, 16), slab)

    def to_owner(placed, here, send, recv, k, p, c):
        return pltpu.make_async_remote_copy(
            src_ref=placed.at[c, pl.ds(pl.multiple_of(p * slab, 16), slab)],
            dst_ref=here.at[c, mine],
            send_sem=send.at[k, c],
            recv_sem=recv.at[k, c],
            device_id=(d, p),
            device_id_type=MESH,
        )

    def weight_to(w, dst, k, q):
        return pltpu.make_async_remote_copy(
            src_ref=slice_of(dst, d),
            dst_ref=slice_of(dst, d),
            send_sem=weight_send.at[w, k],
            recv_sem=weight_recv.at[w, d],
            device_id=(q, o),
            device_id_type=MESH,
        )

    own_tok = [
        pltpu.make_async_copy(tok_placed.at[c, mine], tok_here.at[c, mine], own_sem.at[c])
        for c in range(parts)
    ]
    own_res = [
        pltpu.make_async_copy(
            res_placed.at[c, mine], res_here.at[c, mine], own_sem.at[parts + c]
        )
        for c in range(parts)
    ]

    weights = [
        [weight_to(w, dst, k, q) for k, q in enumerate(others)]
        for w, dst in enumerate((down_all, up_all))
    ]
    tok_copies = [
        [to_owner(tok_placed, tok_here, tok_send, tok_recv, k, p, c) for k, p in enumerate(peers)]
        for c in range(parts)
    ]
    res_copies = [
        [to_owner(res_placed, res_here, res_send, res_recv, k, p, c) for k, p in enumerate(peers)]
        for c in range(parts)
    ]
    loads[1].wait()
    place(tok_in, tok_placed, 0)
    loads[0].wait()
    pl.semaphore_wait(barrier, len(peers) + len(others))
    for copy in weights[0]:
        copy.start()
    for c in range(parts):
        if c:
            place(tok_in, tok_placed, c)
        for copy in tok_copies[c]:
            copy.start()
        own_tok[c].start()
    loads[2].wait()
    for copy in weights[1]:
        copy.start()
    loads[3].wait()
    for c in range(parts):
        place(res_in, res_placed, c)
        for copy in res_copies[c]:
            copy.start()
        own_res[c].start()

    def weight_arrived(w, dst):
        for q in others:
            pltpu.make_async_remote_copy(
                src_ref=slice_of(dst, q),
                dst_ref=slice_of(dst, q),
                send_sem=weight_send.at[w, 0],
                recv_sem=weight_recv.at[w, q],
                device_id=(q, o),
                device_id_type=MESH,
            ).wait_recv()

    cols = lambda c: slice(c * step, (c + 1) * step)
    fold_row = (lax.broadcasted_iota(jnp.int32, (rows, FOLD * rank), 0) % slab) // cap
    fold_lane = lax.broadcasted_iota(jnp.int32, (rows, FOLD * rank), 1) // rank
    same = (fold_row == fold_lane).astype(F32)

    def folded(total, scale):
        kept = total * same
        both = kept + pltpu.roll(kept, rank, 1)
        both = both.reshape(n_owner, FOLD, cap, FOLD * rank)
        whole = both[:, 0] + both[:, 1]
        whole = jnp.stack([whole, whole], axis=1).reshape(rows, FOLD * rank)
        return (scale * whole * same).astype(BF16)

    weight_arrived(0, down_all)
    total = jnp.zeros((rows, FOLD * rank), F32)
    for c in range(parts):
        for copy in tok_copies[c]:
            copy.wait_recv()
        own_tok[c].wait()
        total = total + dot_rows(tok_here[c], down_all[:, cols(c)])
    hidden = folded(total, 1.0)

    weight_arrived(1, up_all)

    ahead = parts // per

    def grad_to(w, part, heard, q, j):
        return pltpu.make_async_remote_copy(
            src_ref=part.at[
                pl.ds(pl.multiple_of((q // per) * rank, 16), rank),
                pl.ds(pl.multiple_of((q % per) * span + j * step, 128), step),
            ],
            dst_ref=heard.at[d, j],
            send_sem=grad_send.at[w, q, j],
            recv_sem=grad_recv.at[w, d, j],
            device_id=(q, o),
            device_id_type=MESH,
        )

    def send_piece(w, part, heard, c):
        for q in range(c // ahead, n_dp, per):

            @pl.when(d != q)
            def _():
                grad_to(w, part, heard, q, c % ahead).start()

    loss_part[...] = jnp.zeros((rows, 128), F32)
    total = jnp.zeros((rows, FOLD * rank), F32)
    for c in range(parts):
        for copy in res_copies[c]:
            copy.wait_recv()
        own_res[c].wait()
        up_c = up_all[:, cols(c)]
        added = (adapter_scale * jnp.dot(hidden, up_c, preferred_element_type=F32)).astype(BF16)
        shifted = res_here[c].astype(F32) + added.astype(F32)
        square = shifted * shifted
        lanes = square[:, :128]
        for j in range(1, step // 128):
            lanes = lanes + square[:, j * 128 : (j + 1) * 128]
        loss_part[...] += lanes
        cotangent = shifted.astype(BF16)
        total = total + dot_rows(cotangent, up_c)
        up_c_grad = adapter_scale * dot_sum(hidden, cotangent)
        up_sum[:, cols(c)] = up_c_grad
        up_part[:, cols(c)] = up_c_grad.astype(BF16)
        send_piece(0, up_part, up_heard, c)
    hidden_grad = folded(total, adapter_scale)

    for c in range(parts):
        down_c_grad = dot_sum(hidden_grad, tok_here[c])
        down_sum[:, cols(c)] = down_c_grad
        down_part[:, cols(c)] = down_c_grad.astype(BF16)
        send_piece(1, down_part, down_heard, c)

    def loss_to(k, p):
        return pltpu.make_async_remote_copy(
            src_ref=loss_part.at[pl.ds(pl.multiple_of(p * slab, 8), slab)],
            dst_ref=loss_heard.at[mine],
            send_sem=loss_send.at[k],
            recv_sem=loss_recv.at[k],
            device_id=(d, p),
            device_id_type=MESH,
        )

    loss_copies = [loss_to(k, p) for k, p in enumerate(peers)]
    for copy in loss_copies:
        copy.start()
    loss_heard[mine, :] = loss_part[mine, :]

    def finish(w, heard, summed, out):
        for j in range(ahead):
            for q in others:
                pltpu.make_async_remote_copy(
                    src_ref=heard.at[q, j],
                    dst_ref=heard.at[q, j],
                    send_sem=grad_send.at[w, q, j],
                    recv_sem=grad_recv.at[w, q, j],
                    device_id=(q, o),
                    device_id_type=MESH,
                ).wait_recv()
            grad = summed[
                pl.ds(pl.multiple_of((d // per) * rank, 16), rank),
                pl.ds(pl.multiple_of((d % per) * span + j * step, 128), step),
            ]
            for q in others:
                grad = grad + heard[q, j].astype(F32)
            out[:, j * step : (j + 1) * step] = grad

    finish(0, up_heard, up_sum, up_out)

    for copy in loss_copies:
        copy.wait_recv()
    sums = jnp.sum(loss_heard[...], axis=1, keepdims=True)
    loss_out[...] = jnp.sum(home * sums, axis=0, keepdims=True)

    finish(1, down_heard, down_sum, down_out)

    for group in weights + tok_copies + res_copies + [loss_copies]:
        for copy in group:
            copy.wait_send()
    for w, part, heard in ((0, up_part, up_heard), (1, down_part, down_heard)):
        for q in others:
            for j in range(ahead):
                grad_to(w, part, heard, q, j).wait_send()


def kernel_body(
    n_dp,
    n_owner,
    cap,
    tokens,
    residual,
    token_adapter_index,
    adapter_down_weight,
    adapter_up_weight,
    down_moment_first,
    down_moment_second,
    up_moment_first,
    up_moment_second,
):
    toks, width = tokens.shape
    _, rank, span = adapter_down_weight.shape
    half, parts = width // FOLD, 8
    step = half // parts
    pieces = span // step
    slab = FOLD * cap
    rows = n_owner * slab
    dma = pltpu.SemaphoreType.DMA
    down_grad, up_grad, row_loss = pl.pallas_call(
        functools.partial(kernel, (n_dp, n_owner, cap, rank, parts)),
        out_shape=(
            jax.ShapeDtypeStruct((rank, span), F32),
            jax.ShapeDtypeStruct((rank, span), F32),
            jax.ShapeDtypeStruct((1, toks), F32),
        ),
        in_specs=[pl.BlockSpec(memory_space=pltpu.VMEM)]
        + [pl.BlockSpec(memory_space=pltpu.HBM)] * 4,
        out_specs=[pl.BlockSpec(memory_space=pltpu.VMEM)] * 3,
        scratch_shapes=[
            pltpu.VMEM((toks, width), BF16),
            pltpu.VMEM((toks, width), BF16),
            pltpu.VMEM((parts, rows, step), BF16),
            pltpu.VMEM((parts, rows, step), BF16),
            pltpu.VMEM((parts, rows, step), BF16),
            pltpu.VMEM((parts, rows, step), BF16),
            pltpu.VMEM((FOLD * rank, half), BF16),
            pltpu.VMEM((FOLD * rank, half), BF16),
            pltpu.VMEM((FOLD * rank, half), F32),
            pltpu.VMEM((FOLD * rank, half), F32),
            pltpu.VMEM((FOLD * rank, half), BF16),
            pltpu.VMEM((FOLD * rank, half), BF16),
            pltpu.VMEM((n_dp, pieces, rank, step), BF16),
            pltpu.VMEM((n_dp, pieces, rank, step), BF16),
            pltpu.VMEM((rows, 128), F32),
            pltpu.VMEM((rows, 128), F32),
            dma((n_owner - 1, parts)),
            dma((n_owner - 1, parts)),
            dma((n_owner - 1, parts)),
            dma((n_owner - 1, parts)),
            dma((2, n_dp)),
            dma((2, n_dp)),
            dma((2, n_dp, pieces)),
            dma((2, n_dp, pieces)),
            dma((n_owner - 1,)),
            dma((n_owner - 1,)),
            dma((2 * parts,)),
            dma((4,)),
        ],
        compiler_params=pltpu.CompilerParams(
            collective_id=0, has_side_effects=True, vmem_limit_bytes=52 * 2**20
        ),
        name="step",
    )(
        token_adapter_index.reshape(1, toks),
        tokens,
        residual,
        adapter_down_weight[0],
        adapter_up_weight[0],
    )
    down_update = adam_update(down_grad[None], down_moment_first, down_moment_second)
    up_update = adam_update(up_grad[None], up_moment_first, up_moment_second)
    return (down_update, up_update, (0.5 / width) * row_loss[0])


def solution(mesh):
    n_dp, n_owner = mesh.shape["dp"], mesh.shape["owner"]

    def body(*arrays):
        toks = arrays[0].shape[0]
        cap = max(2, 3 * toks // (2 * n_owner))
        if cap % 8 == 0 and FOLD * cap % 16 == 0 and n_dp % FOLD == 0 and FOLD * 2 == n_dp:
            return kernel_body(n_dp, n_owner, cap, *arrays)
        return plain_body(*arrays)

    return jax.shard_map(
        body,
        mesh=mesh,
        in_specs=(
            P(("dp", "owner"), None),
            P(("dp", "owner"), None),
            P(("dp", "owner"), None),
            P("owner", None, "dp"),
            P("owner", None, "dp"),
            P("owner", None, "dp"),
            P("owner", None, "dp"),
            P("owner", None, "dp"),
            P("owner", None, "dp"),
        ),
        out_specs=(P("owner", None, "dp"), P("owner", None, "dp"), P(("dp", "owner"))),
        check_vma=False,
    )
```

```python
import functools

import jax
import jax.numpy as jnp
from jax import lax
from jax.experimental import pallas as pl
from jax.experimental.pallas import tpu as pltpu
from jax.sharding import PartitionSpec as P

adapter_scale = 0.5
adam_eps = 1e-08


def adam_update(grad, first, second):
    first_new = 0.9 * first.astype(jnp.float32) + 0.1 * grad
    second_new = 0.95 * second.astype(jnp.float32) + 0.05 * grad * grad
    return first_new / (jnp.sqrt(second_new) + adam_eps)


def plain_body(
    tokens,
    residual,
    token_adapter_index,
    adapter_down_weight,
    adapter_up_weight,
    down_moment_first,
    down_moment_second,
    up_moment_first,
    up_moment_second,
):
    owner_index = lax.axis_size("owner")
    tok_rows = tokens.shape[0]
    model_width_value = tokens.shape[1]
    column_span = adapter_down_weight.shape[2]
    slot_capacity = max(2, 3 * tok_rows // (2 * owner_index))
    route_ids = token_adapter_index[:, 0]
    member = (route_ids[:, None] == jnp.arange(owner_index, dtype=jnp.int32)[None, :]).astype(
        jnp.int32
    )
    earlier = jnp.tril(jnp.ones((tok_rows, tok_rows), jnp.bfloat16), -1)
    before = jnp.dot(
        earlier, member.astype(jnp.bfloat16), preferred_element_type=jnp.float32
    ).astype(jnp.int32)
    within = jnp.sum(before * member, axis=1)
    target = route_ids * slot_capacity + within
    dispatch = (
        jnp.arange(owner_index * slot_capacity, dtype=jnp.int32)[:, None] == target[None, :]
    ).astype(jnp.bfloat16)

    def placed_rows(row_block):
        return jnp.dot(dispatch, row_block, preferred_element_type=jnp.float32).astype(jnp.bfloat16)

    down_full, up_weight_whole = (
        lax.all_gather(adapter_down_weight, "dp", axis=2, tiled=True),
        lax.all_gather(adapter_up_weight, "dp", axis=2, tiled=True),
    )
    down_full = down_full[0]
    up_weight_whole = up_weight_whole[0]

    def spread(row_block):
        return placed_rows(row_block).reshape(owner_index, slot_capacity, model_width_value)

    arrived = lax.all_to_all(
        spread(tokens), "owner", split_axis=0, concat_axis=0, tiled=True
    ).reshape(owner_index * slot_capacity, model_width_value)
    hidden_state = lax.dot_general(
        arrived, down_full, (((1,), (1,)), ((), ())), preferred_element_type=jnp.float32
    ).astype(jnp.bfloat16)
    adapter_output = (
        adapter_scale * jnp.dot(hidden_state, up_weight_whole, preferred_element_type=jnp.float32)
    ).astype(jnp.bfloat16)
    hidden_state, adapter_output = (hidden_state, adapter_output)
    returned = lax.all_to_all(
        adapter_output.reshape(owner_index, slot_capacity, model_width_value),
        "owner",
        split_axis=0,
        concat_axis=0,
        tiled=True,
    )
    returned = returned.reshape(owner_index * slot_capacity, model_width_value)
    adapter_home_index = lax.dot_general(
        dispatch, returned, (((0,), (0,)), ((), ())), preferred_element_type=jnp.float32
    )
    shifted_index = residual.astype(jnp.float32) + adapter_home_index
    token_loss = jnp.mean(0.5 * shifted_index * shifted_index, axis=1)
    output_gradient = lax.all_to_all(
        spread(shifted_index.astype(jnp.bfloat16)), "owner", split_axis=0, concat_axis=0, tiled=True
    )
    output_gradient = output_gradient.reshape(owner_index * slot_capacity, model_width_value)
    up_gradient = adapter_scale * lax.dot_general(
        hidden_state, output_gradient, (((0,), (0,)), ((), ())), preferred_element_type=jnp.float32
    )
    hidden_gradient = (
        adapter_scale
        * lax.dot_general(
            output_gradient,
            up_weight_whole,
            (((1,), (1,)), ((), ())),
            preferred_element_type=jnp.float32,
        )
    ).astype(jnp.bfloat16)
    down_grad = lax.dot_general(
        hidden_gradient, arrived, (((0,), (0,)), ((), ())), preferred_element_type=jnp.float32
    )
    summed_down, summed_up = lax.psum((down_grad, up_gradient), "dp")
    offset = lax.axis_index("dp") * column_span
    down_share = lax.dynamic_slice_in_dim(summed_down, offset, column_span, 1)
    up_share = lax.dynamic_slice_in_dim(summed_up, offset, column_span, 1)
    down_update = adam_update(down_share, down_moment_first[0], down_moment_second[0])
    up_update = adam_update(up_share, up_moment_first[0], up_moment_second[0])
    return (down_update[None], up_update[None], token_loss)


MESH = pl.DeviceIdType.MESH
F32, BF16 = jnp.float32, jnp.bfloat16
FOLD = 2


def dot_rows(a, b):
    return lax.dot_general(a, b, (((1,), (1,)), ((), ())), preferred_element_type=F32)


def dot_sum(a, b):
    return lax.dot_general(a, b, (((0,), (0,)), ((), ())), preferred_element_type=F32)


def kernel(
    sizes,
    ids_ref,
    tok_ref,
    res_ref,
    down_ref,
    up_ref,
    down_out,
    up_out,
    loss_out,
    tok_in,
    res_in,
    tok_placed,
    res_placed,
    tok_here,
    res_here,
    down_all,
    up_all,
    up_sum,
    down_sum,
    up_part,
    up_heard,
    near_part,
    near_heard,
    far_part,
    far_heard,
    loss_part,
    loss_heard,
    tok_send,
    tok_recv,
    res_send,
    res_recv,
    weight_send,
    weight_recv,
    grad_send,
    grad_recv,
    loss_send,
    loss_recv,
    own_sem,
    in_sem,
    relay_send,
    relay_recv,
):
    n_dp, n_owner, cap, rank, parts = sizes
    slab = FOLD * cap
    rows = n_owner * slab
    toks, width = tok_ref.shape
    half = width // FOLD
    span = width // n_dp
    step = half // parts
    per = half // span
    d, o = lax.axis_index("dp"), lax.axis_index("owner")

    def flipped(k):
        peer, bit = 0, 1
        while bit < n_owner:
            own = (o // bit) % 2
            peer = peer + bit * ((own + (k // bit) % 2) % 2)
            bit *= 2
        return peer

    near = sorted(range(1, n_owner), key=lambda k: (k % 2, -k))
    peers = [flipped(k) for k in near]
    others = [lax.rem(d + k, n_dp) for k in range(1, n_dp)]

    def slice_of(ref, q):
        return ref.at[
            pl.ds(pl.multiple_of((q // per) * rank, 16), rank),
            pl.ds(pl.multiple_of((q % per) * span, 128), span),
        ]

    barrier = pltpu.get_barrier_semaphore()
    for p in peers:
        pl.semaphore_signal(barrier, inc=1, device_id=(d, p), device_id_type=MESH)
    for q in others:
        pl.semaphore_signal(barrier, inc=1, device_id=(q, o), device_id_type=MESH)

    loads = [
        pltpu.make_async_copy(src, dst, in_sem.at[i])
        for i, (src, dst) in enumerate(
            (
                (down_ref, slice_of(down_all, d)),
                (tok_ref, tok_in),
                (up_ref, slice_of(up_all, d)),
                (res_ref, res_in),
            )
        )
    ]
    for load in loads:
        load.start()

    ids = ids_ref[...]
    member = (lax.broadcasted_iota(jnp.int32, (n_owner, toks), 0) == ids).astype(F32)
    upper = (
        lax.broadcasted_iota(jnp.int32, (toks, toks), 0)
        < lax.broadcasted_iota(jnp.int32, (toks, toks), 1)
    ).astype(F32)
    before = jnp.dot(member.astype(BF16), upper.astype(BF16), preferred_element_type=F32)
    within = jnp.sum(before * member, axis=0, keepdims=True)
    target = ids.astype(F32) * float(slab) + within
    row = lax.broadcasted_iota(jnp.int32, (rows, toks), 0).astype(F32)
    first_half = (row == target).astype(F32)
    second_half = (row == target + float(cap)).astype(F32)
    home = first_half + second_half
    dispatch = jnp.concatenate([first_half.astype(BF16), second_half.astype(BF16)], axis=1)

    def place(src, dst, c):
        two = jnp.concatenate(
            [src[:, c * step : (c + 1) * step], src[:, half + c * step : half + (c + 1) * step]],
            axis=0,
        )
        dst[c] = jnp.dot(dispatch, two, preferred_element_type=F32).astype(BF16)

    mine = pl.ds(pl.multiple_of(o * slab, 16), slab)

    def to_owner(placed, here, send, recv, k, p, c):
        return pltpu.make_async_remote_copy(
            src_ref=placed.at[c, pl.ds(pl.multiple_of(p * slab, 16), slab)],
            dst_ref=here.at[c, mine],
            send_sem=send.at[k, c],
            recv_sem=recv.at[k, c],
            device_id=(d, p),
            device_id_type=MESH,
        )

    def weight_to(w, dst, k, q):
        return pltpu.make_async_remote_copy(
            src_ref=slice_of(dst, d),
            dst_ref=slice_of(dst, d),
            send_sem=weight_send.at[w, k],
            recv_sem=weight_recv.at[w, d],
            device_id=(q, o),
            device_id_type=MESH,
        )

    own_tok = [
        pltpu.make_async_copy(tok_placed.at[c, mine], tok_here.at[c, mine], own_sem.at[c])
        for c in range(parts)
    ]
    own_res = [
        pltpu.make_async_copy(
            res_placed.at[c, mine], res_here.at[c, mine], own_sem.at[parts + c]
        )
        for c in range(parts)
    ]

    weights = [
        [weight_to(w, dst, k, q) for k, q in enumerate(others)]
        for w, dst in enumerate((down_all, up_all))
    ]
    tok_copies = [
        [to_owner(tok_placed, tok_here, tok_send, tok_recv, k, p, c) for k, p in enumerate(peers)]
        for c in range(parts)
    ]
    res_copies = [
        [to_owner(res_placed, res_here, res_send, res_recv, k, p, c) for k, p in enumerate(peers)]
        for c in range(parts)
    ]
    loads[1].wait()
    place(tok_in, tok_placed, 0)
    loads[0].wait()
    pl.semaphore_wait(barrier, len(peers) + len(others))
    for copy in weights[0]:
        copy.start()
    for c in range(parts):
        if c:
            place(tok_in, tok_placed, c)
        for copy in tok_copies[c]:
            copy.start()
        own_tok[c].start()
    loads[2].wait()
    for copy in weights[1]:
        copy.start()
    loads[3].wait()
    for c in range(parts):
        place(res_in, res_placed, c)
        for copy in res_copies[c]:
            copy.start()
        own_res[c].start()

    def weight_arrived(w, dst):
        for q in others:
            pltpu.make_async_remote_copy(
                src_ref=slice_of(dst, q),
                dst_ref=slice_of(dst, q),
                send_sem=weight_send.at[w, 0],
                recv_sem=weight_recv.at[w, q],
                device_id=(q, o),
                device_id_type=MESH,
            ).wait_recv()

    cols = lambda c: slice(c * step, (c + 1) * step)
    fold_row = (lax.broadcasted_iota(jnp.int32, (rows, FOLD * rank), 0) % slab) // cap
    fold_lane = lax.broadcasted_iota(jnp.int32, (rows, FOLD * rank), 1) // rank
    same = (fold_row == fold_lane).astype(F32)

    def folded(total, scale):
        kept = total * same
        both = kept + pltpu.roll(kept, rank, 1)
        both = both.reshape(n_owner, FOLD, cap, FOLD * rank)
        whole = both[:, 0] + both[:, 1]
        whole = jnp.stack([whole, whole], axis=1).reshape(rows, FOLD * rank)
        return (scale * whole * same).astype(BF16)

    weight_arrived(0, down_all)
    total = jnp.zeros((rows, FOLD * rank), F32)
    for c in range(parts):
        for copy in tok_copies[c]:
            copy.wait_recv()
        own_tok[c].wait()
        total = total + dot_rows(tok_here[c], down_all[:, cols(c)])
    hidden = folded(total, 1.0)

    weight_arrived(1, up_all)

    ahead = parts // per

    def grad_to(w, part, heard, q, j):
        return pltpu.make_async_remote_copy(
            src_ref=part.at[
                pl.ds(pl.multiple_of((q // per) * rank, 16), rank),
                pl.ds(pl.multiple_of((q % per) * span + j * step, 128), step),
            ],
            dst_ref=heard.at[d, j],
            send_sem=grad_send.at[w, q, j],
            recv_sem=grad_recv.at[w, d, j],
            device_id=(q, o),
            device_id_type=MESH,
        )

    def send_piece(w, part, heard, c):
        for q in range(c // ahead, n_dp, per):

            @pl.when(d != q)
            def _():
                grad_to(w, part, heard, q, c % ahead).start()

    loss_part[...] = jnp.zeros((rows, 128), F32)
    total = jnp.zeros((rows, FOLD * rank), F32)
    for c in range(parts):
        for copy in res_copies[c]:
            copy.wait_recv()
        own_res[c].wait()
        up_c = up_all[:, cols(c)]
        added = (adapter_scale * jnp.dot(hidden, up_c, preferred_element_type=F32)).astype(BF16)
        shifted = res_here[c].astype(F32) + added.astype(F32)
        square = shifted * shifted
        lanes = square[:, :128]
        for j in range(1, step // 128):
            lanes = lanes + square[:, j * 128 : (j + 1) * 128]
        loss_part[...] += lanes
        cotangent = shifted.astype(BF16)
        total = total + dot_rows(cotangent, up_c)
        up_c_grad = adapter_scale * dot_sum(hidden, cotangent)
        up_sum[:, cols(c)] = up_c_grad
        up_part[:, cols(c)] = up_c_grad.astype(BF16)
        send_piece(0, up_part, up_heard, c)
    hidden_grad = folded(total, adapter_scale)

    side = d % 2
    partner, far = d + 1 - 2 * side, lax.rem(d + 2, n_dp)

    def relay(i, src, dst, stage, q):
        return pltpu.make_async_remote_copy(
            src_ref=src.at[i],
            dst_ref=dst.at[i],
            send_sem=relay_send.at[stage, i],
            recv_sem=relay_recv.at[stage, i],
            device_id=(q, o),
            device_id_type=MESH,
        )

    near_copies = [relay(i, near_part, near_heard, 0, partner) for i in range(ahead)]
    far_copies = [relay(i, far_part, far_heard, 1, far) for i in range(ahead)]
    for i in range(ahead):
        near_part[i] = dot_sum(hidden_grad, tok_here[(1 - side) * ahead + i]).astype(BF16)
        near_copies[i].start()
    for i in range(ahead):
        down_sum[i] = dot_sum(hidden_grad, tok_here[side * ahead + i])

    def loss_to(k, p):
        return pltpu.make_async_remote_copy(
            src_ref=loss_part.at[pl.ds(pl.multiple_of(p * slab, 8), slab)],
            dst_ref=loss_heard.at[mine],
            send_sem=loss_send.at[k],
            recv_sem=loss_recv.at[k],
            device_id=(d, p),
            device_id_type=MESH,
        )

    loss_copies = [loss_to(k, p) for k, p in enumerate(peers)]
    for copy in loss_copies:
        copy.start()
    loss_heard[mine, :] = loss_part[mine, :]

    def finish(w, heard, summed, out):
        for j in range(ahead):
            for q in others:
                pltpu.make_async_remote_copy(
                    src_ref=heard.at[q, j],
                    dst_ref=heard.at[q, j],
                    send_sem=grad_send.at[w, q, j],
                    recv_sem=grad_recv.at[w, q, j],
                    device_id=(q, o),
                    device_id_type=MESH,
                ).wait_recv()
            grad = summed[
                pl.ds(pl.multiple_of((d // per) * rank, 16), rank),
                pl.ds(pl.multiple_of((d % per) * span + j * step, 128), step),
            ]
            for q in others:
                grad = grad + heard[q, j].astype(F32)
            out[:, j * step : (j + 1) * step] = grad

    for i in range(ahead):
        near_copies[i].wait_recv()
        down_sum[i] += near_heard[i].astype(F32)
        far_row = pl.multiple_of((far // per) * rank, 16)
        far_part[i] = down_sum[i, pl.ds(far_row, rank), :].astype(BF16)
        far_copies[i].start()

    finish(0, up_heard, up_sum, up_out)

    for copy in loss_copies:
        copy.wait_recv()
    sums = jnp.sum(loss_heard[...], axis=1, keepdims=True)
    loss_out[...] = jnp.sum(home * sums, axis=0, keepdims=True)

    for i in range(ahead):
        far_copies[i].wait_recv()
        own_row = pl.multiple_of((d // per) * rank, 16)
        own = down_sum[i, pl.ds(own_row, rank), :]
        down_out[:, i * step : (i + 1) * step] = own + far_heard[i].astype(F32)

    for group in weights + tok_copies + res_copies + [loss_copies, near_copies, far_copies]:
        for copy in group:
            copy.wait_send()
    for w, part, heard in ((0, up_part, up_heard),):
        for q in others:
            for j in range(ahead):
                grad_to(w, part, heard, q, j).wait_send()


def kernel_body(
    n_dp,
    n_owner,
    cap,
    tokens,
    residual,
    token_adapter_index,
    adapter_down_weight,
    adapter_up_weight,
    down_moment_first,
    down_moment_second,
    up_moment_first,
    up_moment_second,
):
    toks, width = tokens.shape
    _, rank, span = adapter_down_weight.shape
    half, parts = width // FOLD, 8
    step = half // parts
    pieces = span // step
    slab = FOLD * cap
    rows = n_owner * slab
    dma = pltpu.SemaphoreType.DMA
    down_grad, up_grad, row_loss = pl.pallas_call(
        functools.partial(kernel, (n_dp, n_owner, cap, rank, parts)),
        out_shape=(
            jax.ShapeDtypeStruct((rank, span), F32),
            jax.ShapeDtypeStruct((rank, span), F32),
            jax.ShapeDtypeStruct((1, toks), F32),
        ),
        in_specs=[pl.BlockSpec(memory_space=pltpu.VMEM)]
        + [pl.BlockSpec(memory_space=pltpu.HBM)] * 4,
        out_specs=[pl.BlockSpec(memory_space=pltpu.VMEM)] * 3,
        scratch_shapes=[
            pltpu.VMEM((toks, width), BF16),
            pltpu.VMEM((toks, width), BF16),
            pltpu.VMEM((parts, rows, step), BF16),
            pltpu.VMEM((parts, rows, step), BF16),
            pltpu.VMEM((parts, rows, step), BF16),
            pltpu.VMEM((parts, rows, step), BF16),
            pltpu.VMEM((FOLD * rank, half), BF16),
            pltpu.VMEM((FOLD * rank, half), BF16),
            pltpu.VMEM((FOLD * rank, half), F32),
            pltpu.VMEM((pieces, FOLD * rank, step), F32),
            pltpu.VMEM((FOLD * rank, half), BF16),
            pltpu.VMEM((n_dp, pieces, rank, step), BF16),
            pltpu.VMEM((pieces, FOLD * rank, step), BF16),
            pltpu.VMEM((pieces, FOLD * rank, step), BF16),
            pltpu.VMEM((pieces, rank, step), BF16),
            pltpu.VMEM((pieces, rank, step), BF16),
            pltpu.VMEM((rows, 128), F32),
            pltpu.VMEM((rows, 128), F32),
            dma((n_owner - 1, parts)),
            dma((n_owner - 1, parts)),
            dma((n_owner - 1, parts)),
            dma((n_owner - 1, parts)),
            dma((2, n_dp)),
            dma((2, n_dp)),
            dma((2, n_dp, pieces)),
            dma((2, n_dp, pieces)),
            dma((n_owner - 1,)),
            dma((n_owner - 1,)),
            dma((2 * parts,)),
            dma((4,)),
            dma((2, pieces)),
            dma((2, pieces)),
        ],
        compiler_params=pltpu.CompilerParams(
            collective_id=0, has_side_effects=True, vmem_limit_bytes=52 * 2**20
        ),
        name="step",
    )(
        token_adapter_index.reshape(1, toks),
        tokens,
        residual,
        adapter_down_weight[0],
        adapter_up_weight[0],
    )
    down_update = adam_update(down_grad[None], down_moment_first, down_moment_second)
    up_update = adam_update(up_grad[None], up_moment_first, up_moment_second)
    return (down_update, up_update, (0.5 / width) * row_loss[0])


def solution(mesh):
    n_dp, n_owner = mesh.shape["dp"], mesh.shape["owner"]

    def body(*arrays):
        toks = arrays[0].shape[0]
        cap = max(2, 3 * toks // (2 * n_owner))
        if cap % 8 == 0 and FOLD * cap % 16 == 0 and n_dp % FOLD == 0 and FOLD * 2 == n_dp:
            return kernel_body(n_dp, n_owner, cap, *arrays)
        return plain_body(*arrays)

    return jax.shard_map(
        body,
        mesh=mesh,
        in_specs=(
            P(("dp", "owner"), None),
            P(("dp", "owner"), None),
            P(("dp", "owner"), None),
            P("owner", None, "dp"),
            P("owner", None, "dp"),
            P("owner", None, "dp"),
            P("owner", None, "dp"),
            P("owner", None, "dp"),
            P("owner", None, "dp"),
        ),
        out_specs=(P("owner", None, "dp"), P("owner", None, "dp"), P(("dp", "owner"))),
        check_vma=False,
    )
```
